256 devices in a mesh: row: 16 (over y, z_hi, core), col: 16 (over z_lo, x).
Axes of the slice: x: 4, y: 4, z: 8 (z_hi: 2, z_lo: 4; z = z_hi * 4 + z_lo), core: 2. Of those that a mesh axis runs over, the one named last changes fastest.
Arguments:
- amplitudes: bfloat16 [8, 1024, 1024], P(None, 'col'), may hold values from -6 to 6
- integrals: bfloat16 [16, 16, 3, 1024, 1024], P('row', 'col'), may hold values from -0.1875 to 0.1875
- labels: int32 [16], replicated, may hold values from 0 to 7, as said below
- slab_list: int32 [8, 2], replicated, may hold values from 0 to 15, as said below
- block_mask: int32 [16, 16], replicated, may hold values 0 or 1
Outputs:
- residual: float32 [1024, 512, 512], P('col', 'row')
The draws below stay inside these ranges and needn't reach their ends.
Inputs may be any that keep to these rules, and one draw needn't show every extreme that they name: Each of the 8 irreps labels exactly 2 blocks. `slab_list`: the listed block pairs are distinct; exactly 3 of them have symmetry 0 and no symmetry has more than 3.
All inputs are finite; a program needn't handle non-finite values.
Results may differ from the reference program's by a relative error of at most 0.0029.
Values may be sent and summed in bfloat16 or wider, within the bound.
No kernel may reach another device: no remote copies, remote signals or barrier semaphores. Data moves between devices by JAX's collectives and lax.ppermute only.
A program may use at most 128 MiB of HBM per device.

```python
import jax
import jax.numpy as jnp
from jax import lax

BLK = 32
NBLK = 16
NVIR = 512
PAIRS = 1024
NSL = 8
CAP = 3


def draw_shared(key):
    keys = jax.random.split(key, 4)
    shuffled = jax.random.permutation(keys[0], NBLK)
    labels = (shuffled % 8).astype(jnp.int32)
    pair_sym = jnp.bitwise_xor(labels[:, None], labels[None, :]).reshape(NBLK * NBLK)
    scores = jax.random.permutation(keys[1], NBLK * NBLK).astype(jnp.int32)
    candidates = jnp.stack([jnp.argsort(scores + NBLK * NBLK * (pair_sym != sym_value).astype(jnp.int32), stable=True) for sym_value in range(8)]).astype(jnp.int32)
    offset = jax.random.randint(keys[2], (), 0, 7).astype(jnp.int32)
    extra = NSL - CAP
    others = extra // 7 + ((jnp.arange(7, dtype=jnp.int32) - offset) % 7 < extra % 7).astype(jnp.int32)
    counts = jnp.concatenate([jnp.array([CAP], dtype=jnp.int32), others])
    cumulative = jnp.cumsum(counts)
    position = jnp.arange(NSL, dtype=jnp.int32)
    slab_sym = jnp.sum((position[:, None] >= cumulative[None, :]).astype(jnp.int32), axis=1)
    within = position - (cumulative[slab_sym] - counts[slab_sym])
    chosen_ids = candidates[slab_sym, within]
    reorder = jax.random.permutation(keys[3], NSL)
    chosen_ids = chosen_ids[reorder]
    slabs = jnp.stack([chosen_ids // NBLK, chosen_ids % NBLK], axis=1).astype(jnp.int32)
    return (labels, slabs)


def draw_labels(key, part):
    shared = draw_shared(key)
    return shared[0]


def draw_slab_list(key, part):
    shared = draw_shared(key)
    return shared[1]


def with_ends(entries, key, low, largest):
    longest = entries.shape.index(max(entries.shape))
    spots = []
    for shift in (0, 1):
        where = [jax.random.randint(jax.random.fold_in(key, axis), (), 0, length) for axis, length in enumerate(entries.shape)]
        where[longest] = (where[longest] + shift) % entries.shape[longest]
        spots.append(tuple(where))
    return entries.at[spots[0]].set(low).at[spots[1]].set(largest)


def steps_of(stream_key, dims, shards, low, high):
    level, own = 1.0, jax.random.fold_in(stream_key, 6)
    for axis_at, shards_of in shards:
        draws = jnp.exp(jax.random.uniform(jax.random.fold_in(own, axis_at), (shards_of,), jnp.float32, low / len(shards), high / len(shards)))
        level = level * jnp.repeat(draws, dims[axis_at] // shards_of).reshape([-1 if axis == axis_at else 1 for axis in range(len(dims))])
    return level


def bell_draw(stream_key, extent, scale, reach, cuts=(), held_as=jnp.bfloat16):
    result = scale * jax.random.normal(stream_key, extent, jnp.float32)
    if cuts:
        result = result * steps_of(stream_key, extent, cuts, -0.22, 0.18)
    return jnp.clip(result, -reach, reach).astype(held_as)


def setup_inputs(seed: int = 0) -> dict:
    seeds = jax.random.split(jax.random.key(seed), 6)
    return {
        "amplitudes": bell_draw(seeds[0], (NSL, PAIRS, BLK * BLK), 1.0, 6.0, ((1, 16),)),
        "integrals": bell_draw(seeds[1], (NBLK, NBLK, CAP, BLK * BLK, BLK * BLK), (BLK * BLK) ** -0.5, 0.1875, ((0, 16), (1, 16))),
        "labels": draw_labels(jax.random.fold_in(seeds[5], 71), 0),
        "slab_list": draw_slab_list(jax.random.fold_in(seeds[5], 71), 0),
        "block_mask": with_ends((jax.random.randint(seeds[4], (NBLK, NBLK), 0, 4) < 3).astype(jnp.int32), jax.random.fold_in(seeds[4], 1), 0, 1),
    }


def slot_table(labels, slab_list, block_mask, a_blocks, b_blocks):
    tile_sym = jnp.bitwise_xor(labels[a_blocks][:, None], labels[b_blocks][None, :])
    left_block = slab_list[:, 0]
    right_block = slab_list[:, 1]
    slab_sym = jnp.bitwise_xor(labels[left_block], labels[right_block])
    alive_flag = block_mask[left_block, right_block]
    matches = (slab_sym[None, None, :] == tile_sym[:, :, None]).astype(jnp.int32)
    slot_rank = jnp.cumsum(matches, axis=2) - 1
    slot_range = jnp.arange(CAP, dtype=jnp.int32)
    picked = matches[:, :, None, :] * (slot_rank[:, :, None, :] == slot_range[:, None]).astype(jnp.int32)
    slab_ids = jnp.sum(picked * jnp.arange(NSL, dtype=jnp.int32), axis=3).astype(jnp.int32)
    filled = jnp.sum(picked, axis=3)
    weights = (filled * alive_flag[slab_ids]).astype(jnp.float32)
    return slab_ids, weights


def reference(amplitudes, integrals, labels, slab_list, block_mask):
    blocks = jnp.arange(NBLK, dtype=jnp.int32)
    slab_ids, weights = slot_table(labels, slab_list, block_mask, blocks, blocks)

    def one_row(a_block):
        chosen = jnp.take(amplitudes, slab_ids[a_block], axis=0).astype(jnp.float32)
        chosen = chosen * weights[a_block][:, :, None, None]
        tiles = integrals[a_block].astype(jnp.float32).reshape(NBLK, CAP, BLK, BLK, BLK * BLK)
        summed = jnp.einsum("jkpc,jkxyc->pxjy", chosen, tiles)
        return summed.astype(jnp.bfloat16)

    row_tiles = lax.map(one_row, blocks)
    ladder = jnp.transpose(row_tiles, (1, 0, 2, 3, 4)).reshape(PAIRS, NVIR, NVIR)
    widened = ladder.astype(jnp.float32)
    return widened - jnp.swapaxes(widened, 1, 2)
```

```python
import functools

import jax
import jax.numpy as jnp
import numpy as np
from jax import lax
from jax.experimental import pallas as pl
from jax.experimental.pallas import tpu as pltpu
from jax.sharding import PartitionSpec as P

BLK = 32
NSL = 8
CAP = 3
NB = 16
TILE = BLK * BLK
BF = jnp.bfloat16
F32 = jnp.float32
ANY = pl.BlockSpec(memory_space=pl.ANY)
SMEM = pl.BlockSpec(memory_space=pltpu.SMEM)
VM = pl.BlockSpec(memory_space=pltpu.VMEM)
AXES = ("row", "col")


def hop(array, axis, step):
    pairs = []
    for row in range(NB):
        for col in range(NB):
            y, zh, core, zl, x = row // 4, row // 2 % 2, row % 2, col // 4, col % 4
            z = zh * 4 + zl
            if axis == "x":
                x = (x + step) % 4
            elif axis == "z":
                z = (z + step) % 8
            else:
                core = 1 - core
            to = (y * 4 + z // 4 * 2 + core) * NB + z % 4 * 4 + x
            pairs.append((row * NB + col, to))
    return lax.ppermute(array, AXES, pairs)


def run_copies(copies):
    for copy in copies:
        copy.start()
    for copy in copies:
        copy.wait()


def cut_kernel(place, shard, a0, a1, b0, b1, sems):
    first = lax.rem(place[0], 2) * 32
    copies = []
    for half, dst in ((0, a0), (1, a1), (2, b0), (3, b1)):
        rows = pl.ds(pl.multiple_of(first + half // 2 * 16, 16), 16)
        slabs = pl.ds(half % 2 * 4, 4)
        copies.append(pltpu.make_async_copy(shard.at[slabs, rows, :], dst, sems.at[half]))
    run_copies(copies)


def cut(place, shard):
    piece = jax.ShapeDtypeStruct((4, 16, TILE), BF)
    return pl.pallas_call(
        cut_kernel,
        out_shape=[piece] * 4,
        in_specs=[SMEM, ANY],
        out_specs=[ANY] * 4,
        scratch_shapes=[pltpu.SemaphoreType.DMA((4,))],
        name="cut",
    )(place, shard)


def stack_kernel(*refs):
    sems = refs[-1]
    ins, outs = refs[:16], refs[16:20]
    run_copies(
        [
            pltpu.make_async_copy(ins[i], outs[i // 4].at[i % 4], sems.at[i])
            for i in range(16)
        ]
    )


def stack(pieces):
    piece = jax.ShapeDtypeStruct((4, 4, 16, TILE), BF)
    return pl.pallas_call(
        stack_kernel,
        out_shape=[piece] * 4,
        in_specs=[ANY] * 16,
        out_specs=[ANY] * 4,
        scratch_shapes=[pltpu.SemaphoreType.DMA((16,))],
        name="stack",
    )(*pieces)


def ring(a0, a1, axis):
    a0p, a1m = hop(a0, axis, 1), hop(a1, axis, -1)
    a1p, a0m = hop(a1, axis, 1), hop(a0, axis, -1)
    a0pp, a1mm = hop(a0p, axis, 1), hop(a1m, axis, -1)
    return (a0, a0p, a0m, a0pp), (a1, a1p, a1m, a1mm)


def slots(row, col, labels, slab_list, block_mask):
    sym = lax.bitwise_xor(labels[row], labels[col])
    count = jnp.int32(0)
    ids = [jnp.int32(0)] * CAP
    weights = [jnp.float32(0)] * CAP
    for s in range(NSL):
        left, right = slab_list[s, 0], slab_list[s, 1]
        match = lax.bitwise_xor(labels[left], labels[right]) == sym
        alive = jnp.where(block_mask[left, right] == 1, jnp.float32(1), jnp.float32(0))
        for k in range(CAP):
            here = jnp.logical_and(match, count == k)
            ids[k] = jnp.where(here, jnp.int32(s), ids[k])
            weights[k] = jnp.where(here, alive, weights[k])
        count = count + match.astype(jnp.int32)
    return ids, weights


def choose(ids, col, pieces, target, sems):
    shift = (0, 3, 1, 2)
    zl, x = col // 4, lax.rem(col, 4)
    waits = []
    n = 0
    for part in range(2):
        for outer in range(4):
            for inner in range(4):
                rel_x, rel_z = (inner, outer) if part == 0 else (outer, inner)
                q = lax.rem(zl + shift[rel_z], 4) * 4 + lax.rem(x + shift[rel_x], 4)
                for k in range(CAP):
                    upper = ids[k] >= 4
                    slab = lax.rem(ids[k], 4)
                    pair = [
                        pltpu.make_async_copy(
                            pieces[part][half][outer].at[inner, slab],
                            target(k, q, part),
                            sems.at[n],
                        )
                        for half in range(2)
                    ]

                    @pl.when(upper)
                    def _(copy=pair[1]):
                        copy.start()

                    @pl.when(jnp.logical_not(upper))
                    def _(copy=pair[0]):
                        copy.start()

                    waits.append(pair[0])
                    n += 1
    return waits


def nest(refs):
    return [[refs[(part * 2 + half) * 4 : (part * 2 + half) * 4 + 4] for half in range(2)] for part in range(2)]


def pick_kernel(place, labels, slab_list, block_mask, *refs):
    pieces, out, sems = nest(refs[:16]), refs[16], refs[17]
    row, col = place[0], place[1]
    other = row + 1 - 2 * lax.rem(row, 2)
    ids, _ = slots(other, col, labels, slab_list, block_mask)

    def target(k, q, part):
        return out.at[k, q, pl.ds(part * 16, 16), :]

    for copy in choose(ids, col, pieces, target, sems):
        copy.wait()


def pick(place, labels, slab_list, block_mask, pieces):
    return pl.pallas_call(
        pick_kernel,
        out_shape=jax.ShapeDtypeStruct((CAP, NB, 32, TILE), BF),
        in_specs=[SMEM] * 4 + [ANY] * 16,
        out_specs=ANY,
        scratch_shapes=[pltpu.SemaphoreType.DMA((96,))],
        name="pick",
    )(place, labels, slab_list, block_mask, *pieces)


def ladder_kernel(place, labels, slab_list, block_mask, *refs):
    pieces, met, integrals, out = nest(refs[:16]), refs[16], refs[17], refs[18]
    lhs, rhs, sems, more = refs[19:]
    row, col = place[0], place[1]
    load = [pltpu.make_async_copy(integrals.at[0, 0, k], rhs.at[k], more.at[k]) for k in range(CAP)]
    for copy in load:
        copy.start()
    core = lax.rem(row, 2)
    mine = pl.multiple_of(core * 32, 32)
    theirs = pl.multiple_of(32 - core * 32, 32)
    rest = [
        pltpu.make_async_copy(met.at[k], lhs.at[k, :, pl.ds(theirs, 32), :], more.at[CAP + k])
        for k in range(CAP)
    ]
    for copy in rest:
        copy.start()
    ids, weights = slots(row, col, labels, slab_list, block_mask)

    def target(k, q, part):
        return lhs.at[k, q, pl.ds(mine + part * 16, 16), :]

    waits = choose(ids, col, pieces, target, sems)
    for copy in load + rest + waits:
        copy.wait()

    @pl.loop(0, 4)
    def _(step):
        rows = pl.ds(step * 4, 4)
        total = jnp.zeros((256, TILE), F32)
        for k in range(CAP):
            part = lax.dot_general(
                lhs[k, rows].reshape(256, TILE),
                rhs[k],
                (((1,), (1,)), ((), ())),
                preferred_element_type=F32,
            )
            total = total + weights[k] * part
        out[rows] = total.astype(BF).reshape(4, 64, TILE)


def ladder(place, labels, slab_list, block_mask, pieces, met, integrals):
    return pl.pallas_call(
        ladder_kernel,
        out_shape=jax.ShapeDtypeStruct((NB, 64, TILE), BF),
        in_specs=[SMEM] * 4 + [ANY] * 18,
        out_specs=VM,
        scratch_shapes=[
            pltpu.VMEM((CAP, NB, 64, TILE), BF),
            pltpu.VMEM((CAP, TILE, TILE), BF),
            pltpu.SemaphoreType.DMA((96,)),
            pltpu.SemaphoreType.DMA((2 * CAP,)),
        ],
        compiler_params=pltpu.CompilerParams(vmem_limit_bytes=48 * 2**20),
        cost_estimate=pl.CostEstimate(flops=6 * 2**30, bytes_accessed=20 * 2**20, transcendentals=0),
        name="ladder",
    )(place, labels, slab_list, block_mask, *pieces, met, integrals)


PB = 16


def finish_kernel(own, other, swap, out):
    swapped = lax.dot_general(
        other[...].reshape(NB * PB, TILE),
        swap[...],
        (((1,), (0,)), ((), ())),
        preferred_element_type=F32,
    ).reshape(NB, PB, TILE)
    diff = [own[b].astype(F32) - swapped[b] for b in range(NB)]
    for u in range(BLK):
        out[:, u, :] = jnp.concatenate([d[:, u * BLK : (u + 1) * BLK] for d in diff], axis=1)


def finish(own, other, swap):
    block = pl.BlockSpec((NB, PB, TILE), lambda i: (0, i, 0))
    return pl.pallas_call(
        finish_kernel,
        grid=(64 // PB,),
        out_shape=jax.ShapeDtypeStruct((64, BLK, NB * BLK), F32),
        in_specs=[block, block, pl.BlockSpec((TILE, TILE), lambda i: (0, 0))],
        out_specs=pl.BlockSpec((PB, BLK, NB * BLK), lambda i: (i, 0, 0)),
        compiler_params=pltpu.CompilerParams(vmem_limit_bytes=48 * 2**20),
        name="finish",
    )(own, other, swap)


def swap_matrix():
    source = lax.broadcasted_iota(jnp.int32, (TILE, TILE), 0)
    target = lax.broadcasted_iota(jnp.int32, (TILE, TILE), 1)
    return (source % BLK * BLK + source // BLK == target).astype(BF)


def body(amplitudes, integrals, labels, slab_list, block_mask):
    place = jnp.stack([lax.axis_index("row"), lax.axis_index("col")]).astype(jnp.int32)
    swap = swap_matrix()
    a0, a1, b0, b1 = cut(place, amplitudes)
    low_a, high_a = ring(a0, a1, "x")
    low_b, high_b = ring(b0, b1, "z")
    av0, av1, bv0, bv1 = stack(low_a + high_a + low_b + high_b)
    low_a, high_a = ring(av0, av1, "z")
    low_b, high_b = ring(bv0, bv1, "x")
    pieces = low_a + high_a + low_b + high_b
    met = hop(pick(place, labels, slab_list, block_mask, pieces), "core", 1)
    tile = ladder(place, labels, slab_list, block_mask, pieces, met, integrals)
    own = lax.all_to_all(tile, "col", split_axis=0, concat_axis=0, tiled=True)
    other = lax.all_to_all(own, "row", split_axis=0, concat_axis=0, tiled=True)
    return finish(own, other, swap)


def solution(mesh):
    in_specs = (P(None, "col", None), P("row", "col", None, None, None), P(), P(), P())
    out_specs = P("col", "row", None)
    return jax.shard_map(body, mesh=mesh, in_specs=in_specs, out_specs=out_specs, check_vma=False)
```

```python
import jax
import jax.numpy as jnp
from jax import lax
from jax.experimental import pallas as pl
from jax.experimental.pallas import tpu as pltpu
from jax.sharding import PartitionSpec as P

BLK = 32
NSL = 8
CAP = 3
NB = 16
TILE = BLK * BLK
BF = jnp.bfloat16
F32 = jnp.float32
HBM = pl.BlockSpec(memory_space=pltpu.MemorySpace.HBM)
SMEM = pl.BlockSpec(memory_space=pltpu.SMEM)
VM = pl.BlockSpec(memory_space=pltpu.VMEM)
AXES = ("row", "col")


def hop(array, axis, step):
    pairs = []
    for row in range(NB):
        for col in range(NB):
            y, zh, core, zl, x = row // 4, row // 2 % 2, row % 2, col // 4, col % 4
            z = zh * 4 + zl
            if axis == "x":
                x = (x + step) % 4
            elif axis == "z":
                z = (z + step) % 8
            else:
                core = 1 - core
            to = (y * 4 + z // 4 * 2 + core) * NB + z % 4 * 4 + x
            pairs.append((row * NB + col, to))
    return lax.ppermute(array, AXES, pairs)


def run_copies(copies):
    for copy in copies:
        copy.start()
    for copy in copies:
        copy.wait()


def cut_kernel(place, shard, a0, a1, b0, b1, sems):
    first = lax.rem(place[0], 2) * 32
    copies = []
    for half, dst in ((0, a0), (1, a1), (2, b0), (3, b1)):
        rows = pl.ds(pl.multiple_of(first + half // 2 * 16, 16), 16)
        slabs = pl.ds(half % 2 * 4, 4)
        copies.append(pltpu.make_async_copy(shard.at[slabs, rows, :], dst, sems.at[half]))
    run_copies(copies)


def cut(place, shard):
    piece = jax.ShapeDtypeStruct((4, 16, TILE), BF)
    return pl.pallas_call(
        cut_kernel,
        out_shape=[piece] * 4,
        in_specs=[SMEM, HBM],
        out_specs=[VM] * 4,
        scratch_shapes=[pltpu.SemaphoreType.DMA((4,))],
        name="cut",
    )(place, shard)


def stack_kernel(*refs):
    sems = refs[-1]
    ins, outs = refs[:16], refs[16:20]
    run_copies(
        [
            pltpu.make_async_copy(ins[i], outs[i // 4].at[i % 4], sems.at[i])
            for i in range(16)
        ]
    )


def stack(pieces):
    piece = jax.ShapeDtypeStruct((4, 4, 16, TILE), BF)
    return pl.pallas_call(
        stack_kernel,
        out_shape=[piece] * 4,
        in_specs=[HBM] * 16,
        out_specs=[VM] * 4,
        scratch_shapes=[pltpu.SemaphoreType.DMA((16,))],
        name="stack",
    )(*pieces)


def ring(a0, a1, axis):
    a0p, a1m = hop(a0, axis, 1), hop(a1, axis, -1)
    a1p, a0m = hop(a1, axis, 1), hop(a0, axis, -1)
    a0pp, a1mm = hop(a0p, axis, 1), hop(a1m, axis, -1)
    return (a0, a0p, a0m, a0pp), (a1, a1p, a1m, a1mm)


def slots(row, col, labels, slab_list, block_mask):
    sym = lax.bitwise_xor(labels[row], labels[col])
    count = jnp.int32(0)
    ids = [jnp.int32(0)] * CAP
    weights = [jnp.float32(0)] * CAP
    for s in range(NSL):
        left, right = slab_list[s, 0], slab_list[s, 1]
        match = lax.bitwise_xor(labels[left], labels[right]) == sym
        alive = jnp.where(block_mask[left, right] == 1, jnp.float32(1), jnp.float32(0))
        for k in range(CAP):
            here = jnp.logical_and(match, count == k)
            ids[k] = jnp.where(here, jnp.int32(s), ids[k])
            weights[k] = jnp.where(here, alive, weights[k])
        count = count + match.astype(jnp.int32)
    return ids, weights


def nest(refs):
    return [[refs[(part * 2 + half) * 4 : (part * 2 + half) * 4 + 4] for half in range(2)] for part in range(2)]


def pick_kernel(place, labels, slab_list, block_mask, *refs):
    pieces, outs, held, sems = refs[:16], refs[16:18], refs[18], refs[19]
    copies = [pltpu.make_async_copy(pieces[n], held.at[n // 8, n // 4 % 2, n % 4], sems.at[n]) for n in range(16)]
    for copy in copies:
        copy.start()
    row, col = place[0], place[1]
    zl, x = col // 4, lax.rem(col, 4)
    shift = (0, 3, 1, 2)
    chosen = [
        slots(r, col, labels, slab_list, block_mask)[0]
        for r in (row + 1 - 2 * lax.rem(row, 2), row)
    ]
    for copy in copies:
        copy.wait()
    for ids, out in zip(chosen, outs, strict=True):
        for part in range(2):
            for outer in range(4):
                for inner in range(4):
                    rel_x, rel_z = (inner, outer) if part == 0 else (outer, inner)
                    q = lax.rem(zl + shift[rel_z], 4) * 4 + lax.rem(x + shift[rel_x], 4)
                    for k in range(CAP):
                        out[k, q, part * 16 : part * 16 + 16] = held[
                            part, ids[k] // 4, outer, inner, lax.rem(ids[k], 4)
                        ]


def pick(place, labels, slab_list, block_mask, pieces):
    return pl.pallas_call(
        pick_kernel,
        out_shape=[jax.ShapeDtypeStruct((CAP, NB, 32, TILE), BF)] * 2,
        in_specs=[SMEM] * 4 + [HBM] * 16,
        out_specs=[VM] * 2,
        scratch_shapes=[pltpu.VMEM((2, 2, 4, 4, 4, 16, TILE), BF), pltpu.SemaphoreType.DMA((16,))],
        compiler_params=pltpu.CompilerParams(vmem_limit_bytes=60 * 2**20),
        name="pick",
    )(place, labels, slab_list, block_mask, *pieces)


def multiply(lhs, rhs, weights, store):
    @pl.loop(0, 2)
    def _(step):
        rows = pl.ds(step * 8, 8)
        total = jnp.zeros((256, TILE), F32)
        for k in range(CAP):
            part = lax.dot_general(
                lhs[k, rows].reshape(256, TILE),
                rhs[k],
                (((1,), (1,)), ((), ())),
                preferred_element_type=F32,
            )
            total = total + weights[k] * part
        store(rows, total.astype(BF).reshape(8, 32, TILE))


def own_kernel(place, labels, slab_list, block_mask, mine, integrals, out, lhs, rhs, sems):
    copies = [pltpu.make_async_copy(integrals.at[0, 0, k], rhs.at[k], sems.at[k]) for k in range(CAP)]
    copies += [pltpu.make_async_copy(mine.at[k], lhs.at[k], sems.at[CAP + k]) for k in range(CAP)]
    for copy in copies:
        copy.start()
    _, weights = slots(place[0], place[1], labels, slab_list, block_mask)
    for copy in copies:
        copy.wait()

    def store(rows, value):
        out[rows] = value

    multiply(lhs, rhs, weights, store)


def met_kernel(place, labels, slab_list, block_mask, met, integrals, half, out, lhs, rhs, held, sems):
    copies = [pltpu.make_async_copy(integrals.at[0, 0, k], rhs.at[k], sems.at[k]) for k in range(CAP)]
    copies += [pltpu.make_async_copy(met.at[k], lhs.at[k], sems.at[CAP + k]) for k in range(CAP)]
    copies += [pltpu.make_async_copy(half, held, sems.at[2 * CAP])]
    for copy in copies:
        copy.start()
    core = lax.rem(place[0], 2)
    _, weights = slots(place[0], place[1], labels, slab_list, block_mask)
    for copy in copies:
        copy.wait()
    out[:, pl.ds(pl.multiple_of(core * 32, 32), 32)] = held[...]
    theirs = pl.ds(pl.multiple_of(32 - core * 32, 32), 32)

    def store(rows, value):
        out[rows, theirs] = value

    multiply(lhs, rhs, weights, store)


HALF_COST = pl.CostEstimate(flops=3 * 2**30, bytes_accessed=11 * 2**20, transcendentals=0)
HALF_VMEM = [pltpu.VMEM((CAP, NB, 32, TILE), BF), pltpu.VMEM((CAP, TILE, TILE), BF)]
LARGE = pltpu.CompilerParams(vmem_limit_bytes=60 * 2**20)


def ladder_own(place, labels, slab_list, block_mask, mine, integrals):
    return pl.pallas_call(
        own_kernel,
        out_shape=jax.ShapeDtypeStruct((NB, 32, TILE), BF),
        in_specs=[SMEM] * 4 + [HBM] * 2,
        out_specs=VM,
        scratch_shapes=HALF_VMEM + [pltpu.SemaphoreType.DMA((2 * CAP,))],
        compiler_params=LARGE,
        cost_estimate=HALF_COST,
        name="ladder_own",
    )(place, labels, slab_list, block_mask, mine, integrals)


def ladder_met(place, labels, slab_list, block_mask, met, integrals, half):
    return pl.pallas_call(
        met_kernel,
        out_shape=jax.ShapeDtypeStruct((NB, 64, TILE), BF),
        in_specs=[SMEM] * 4 + [HBM] * 3,
        out_specs=VM,
        scratch_shapes=HALF_VMEM + [pltpu.VMEM((NB, 32, TILE), BF), pltpu.SemaphoreType.DMA((2 * CAP + 1,))],
        compiler_params=LARGE,
        cost_estimate=HALF_COST,
        name="ladder_met",
    )(place, labels, slab_list, block_mask, met, integrals, half)


PB = 16


def finish_kernel(own, other, swap, out):
    swapped = lax.dot_general(
        other[...].reshape(NB * PB, TILE),
        swap[...],
        (((1,), (0,)), ((), ())),
        preferred_element_type=F32,
    ).reshape(NB, PB, TILE)
    diff = [own[b].astype(F32) - swapped[b] for b in range(NB)]
    for u in range(BLK):
        out[:, u, :] = jnp.concatenate([d[:, u * BLK : (u + 1) * BLK] for d in diff], axis=1)


def finish(own, other, swap):
    block = pl.BlockSpec((NB, PB, TILE), lambda i: (0, i, 0))
    return pl.pallas_call(
        finish_kernel,
        grid=(64 // PB,),
        out_shape=jax.ShapeDtypeStruct((64, BLK, NB * BLK), F32),
        in_specs=[block, block, pl.BlockSpec((TILE, TILE), lambda i: (0, 0))],
        out_specs=pl.BlockSpec((PB, BLK, NB * BLK), lambda i: (i, 0, 0)),
        compiler_params=pltpu.CompilerParams(vmem_limit_bytes=48 * 2**20),
        name="finish",
    )(own, other, swap)


def swap_matrix():
    source = lax.broadcasted_iota(jnp.int32, (TILE, TILE), 0)
    target = lax.broadcasted_iota(jnp.int32, (TILE, TILE), 1)
    return (source % BLK * BLK + source // BLK == target).astype(BF)


def body(amplitudes, integrals, labels, slab_list, block_mask):
    place = jnp.stack([lax.axis_index("row"), lax.axis_index("col")]).astype(jnp.int32)
    swap = swap_matrix()
    a0, a1, b0, b1 = cut(place, amplitudes)
    low_a, high_a = ring(a0, a1, "x")
    low_b, high_b = ring(b0, b1, "z")
    av0, av1, bv0, bv1 = stack(low_a + high_a + low_b + high_b)
    low_a, high_a = ring(av0, av1, "z")
    low_b, high_b = ring(bv0, bv1, "x")
    pieces = low_a + high_a + low_b + high_b
    slot_args = (place, labels, slab_list, block_mask)
    other, mine = pick(*slot_args, pieces)
    met = hop(other, "core", 1)
    half = ladder_own(*slot_args, mine, integrals)
    tile = ladder_met(*slot_args, met, integrals, half)
    own = lax.all_to_all(tile, "col", split_axis=0, concat_axis=0, tiled=True)
    other = lax.all_to_all(own, "row", split_axis=0, concat_axis=0, tiled=True)
    return finish(own, other, swap)


def solution(mesh):
    in_specs = (P(None, "col", None), P("row", "col", None, None, None), P(), P(), P())
    out_specs = P("col", "row", None)
    return jax.shard_map(body, mesh=mesh, in_specs=in_specs, out_specs=out_specs, check_vma=False)
```

```python
import jax
import jax.numpy as jnp
from jax import lax
from jax.experimental import pallas as pl
from jax.experimental.pallas import tpu as pltpu
from jax.sharding import PartitionSpec as P

BLK = 32
NSL = 8
CAP = 3
NB = 16
TILE = BLK * BLK
BF = jnp.bfloat16
F32 = jnp.float32
HBM = pl.BlockSpec(memory_space=pltpu.MemorySpace.HBM)
SMEM = pl.BlockSpec(memory_space=pltpu.SMEM)
VM = pl.BlockSpec(memory_space=pltpu.VMEM)
AXES = ("row", "col")
SHIFT = (0, 3, 1, 2)


def hop(array, axis, step):
    pairs = []
    for row in range(NB):
        for col in range(NB):
            y, zh, core, zl, x = row // 4, row // 2 % 2, row % 2, col // 4, col % 4
            z = zh * 4 + zl
            if axis == "x":
                x = (x + step) % 4
            elif axis == "z":
                z = (z + step) % 8
            else:
                core = 1 - core
            to = (y * 4 + z // 4 * 2 + core) * NB + z % 4 * 4 + x
            pairs.append((row * NB + col, to))
    return lax.ppermute(array, AXES, pairs)


def run_copies(copies):
    for copy in copies:
        copy.start()
    for copy in copies:
        copy.wait()


def cut_kernel(place, shard, a0, a1, b0, b1, sems):
    first = lax.rem(place[0], 2) * 32
    copies = []
    for half, dst in ((0, a0), (1, a1), (2, b0), (3, b1)):
        rows = pl.ds(pl.multiple_of(first + half // 2 * 16, 16), 16)
        slabs = pl.ds(half % 2 * 4, 4)
        copies.append(pltpu.make_async_copy(shard.at[slabs, rows, :], dst, sems.at[half]))
    run_copies(copies)


def cut(place, shard):
    piece = jax.ShapeDtypeStruct((4, 16, TILE), BF)
    return pl.pallas_call(
        cut_kernel,
        out_shape=[piece] * 4,
        in_specs=[SMEM, HBM],
        out_specs=[VM] * 4,
        scratch_shapes=[pltpu.SemaphoreType.DMA((4,))],
        name="cut",
    )(place, shard)


def stack_kernel(*refs):
    sems = refs[-1]
    ins, outs = refs[:16], refs[16:20]
    run_copies(
        [
            pltpu.make_async_copy(ins[i], outs[i // 4].at[i % 4], sems.at[i])
            for i in range(16)
        ]
    )


def stack(pieces):
    piece = jax.ShapeDtypeStruct((4, 4, 16, TILE), BF)
    return pl.pallas_call(
        stack_kernel,
        out_shape=[piece] * 4,
        in_specs=[HBM] * 16,
        out_specs=[VM] * 4,
        scratch_shapes=[pltpu.SemaphoreType.DMA((16,))],
        name="stack",
    )(*pieces)


def ring(a0, a1, axis):
    a0p, a1m = hop(a0, axis, 1), hop(a1, axis, -1)
    a1p, a0m = hop(a1, axis, 1), hop(a0, axis, -1)
    a0pp, a1mm = hop(a0p, axis, 1), hop(a1m, axis, -1)
    return (a0, a0p, a0m, a0pp), (a1, a1p, a1m, a1mm)


def slots(row, col, labels, slab_list, block_mask):
    sym = lax.bitwise_xor(labels[row], labels[col])
    count = jnp.int32(0)
    ids = [jnp.int32(0)] * CAP
    weights = [jnp.float32(0)] * CAP
    for s in range(NSL):
        left, right = slab_list[s, 0], slab_list[s, 1]
        match = lax.bitwise_xor(labels[left], labels[right]) == sym
        alive = jnp.where(block_mask[left, right] == 1, jnp.float32(1), jnp.float32(0))
        for k in range(CAP):
            here = jnp.logical_and(match, count == k)
            ids[k] = jnp.where(here, jnp.int32(s), ids[k])
            weights[k] = jnp.where(here, alive, weights[k])
        count = count + match.astype(jnp.int32)
    return ids, weights


def nest(refs):
    return [[refs[(part * 2 + half) * 4 : (part * 2 + half) * 4 + 4] for half in range(2)] for part in range(2)]


def ladder_kernel(place, labels, slab_list, block_mask, *refs):
    pieces, here, there, out = nest(refs[:16]), refs[16], refs[17], refs[18]
    lhs, rhs, acc, sems, more = refs[19:]
    row, col = place[0], place[1]
    core, zl, x = lax.rem(row, 2), col // 4, lax.rem(col, 4)
    tiles = (core, 1 - core)
    stages = []
    for n, source in enumerate((here, there)):
        ids, weights = slots(row + tiles[n] - core, col, labels, slab_list, block_mask)
        stages += [(n, k, source, ids[k], weights[k] > 0) for k in range(CAP)]

    def parts(n, k, slab, half):
        return [
            pltpu.make_async_copy(
                pieces[part][half][outer].at[:, lax.rem(slab, 4)],
                lhs.at[n, k, part, outer],
                sems.at[(n * CAP + k) * 8 + part * 4 + outer],
            )
            for part in range(2)
            for outer in range(4)
        ]

    def start(n, k, source, slab, alive):
        for half in range(2):

            @pl.when(jnp.logical_and(alive, slab // 4 == half))
            def _():
                for copy in parts(n, k, slab, half):
                    copy.start()

        @pl.when(alive)
        def _():
            pltpu.make_async_copy(source.at[0, 0, k], rhs.at[n, k], more.at[n * CAP + k]).start()

    def add(n, k, source, slab, alive):
        @pl.when(alive)
        def _():
            for copy in parts(n, k, slab, 0):
                copy.wait()
            pltpu.make_async_copy(source.at[0, 0, k], rhs.at[n, k], more.at[n * CAP + k]).wait()
            value = lax.dot_general(
                lhs[n, k].reshape(512, TILE),
                rhs[n, k],
                (((1,), (1,)), ((), ())),
                preferred_element_type=F32,
            )
            acc[...] = value if k == 0 else acc[...] + value

        if k == 0:

            @pl.when(jnp.logical_not(alive))
            def _():
                acc[...] = jnp.zeros_like(acc)

    for stage in stages[:2]:
        start(*stage)
    for i, stage in enumerate(stages):
        if i + 2 < len(stages):
            start(*stages[i + 2])
        add(*stage)
        if stage[1] == CAP - 1:
            for part in range(2):
                for outer in range(4):
                    for inner in range(4):
                        rel_x, rel_z = (inner, outer) if part == 0 else (outer, inner)
                        q = lax.rem(zl + SHIFT[rel_z], 4) * 4 + lax.rem(x + SHIFT[rel_x], 4)
                        first = (part * 16 + outer * 4 + inner) * 16
                        out[q, tiles[stage[0]], part * 16 : part * 16 + 16] = acc[first : first + 16].astype(BF)


def ladder(place, labels, slab_list, block_mask, pieces, here, there):
    return pl.pallas_call(
        ladder_kernel,
        out_shape=jax.ShapeDtypeStruct((NB, 2, 32, TILE), BF),
        in_specs=[SMEM] * 4 + [HBM] * 18,
        out_specs=VM,
        scratch_shapes=[
            pltpu.VMEM((2, CAP, 2, 4, 4, 16, TILE), BF),
            pltpu.VMEM((2, CAP, TILE, TILE), BF),
            pltpu.VMEM((512, TILE), F32),
            pltpu.SemaphoreType.DMA((48,)),
            pltpu.SemaphoreType.DMA((2 * CAP,)),
        ],
        compiler_params=pltpu.CompilerParams(vmem_limit_bytes=60 * 2**20),
        cost_estimate=pl.CostEstimate(flops=6 * 2**30, bytes_accessed=22 * 2**20, transcendentals=0),
        name="ladder",
    )(place, labels, slab_list, block_mask, *pieces, here, there)


def rest_kernel(place, own, out, sem):
    copy = pltpu.make_async_copy(own.at[:, 1 - lax.rem(place[0], 2)], out, sem)
    copy.start()
    copy.wait()


def rest(place, own):
    return pl.pallas_call(
        rest_kernel,
        out_shape=jax.ShapeDtypeStruct((NB, 32, TILE), BF),
        in_specs=[SMEM, HBM],
        out_specs=VM,
        scratch_shapes=[pltpu.SemaphoreType.DMA],
        name="rest",
    )(place, own)


PB = 16


def finish_kernel(place, own, met, other, swap, out):
    core = lax.rem(place[0], 2)
    turned = lax.dot_general(
        other[...].reshape(NB * 2 * PB, TILE),
        swap[...],
        (((1,), (0,)), ((), ())),
        preferred_element_type=F32,
    ).reshape(NB, 2, PB, TILE)
    for half in range(2):
        first = core == half
        diff = []
        for b in range(NB):
            straight = jnp.where(first, own[b, core].astype(F32), met[b].astype(F32))
            diff.append(straight - turned[b // 2 * 2 + half, b % 2])
        for u in range(BLK):
            out[half, :, u, :] = jnp.concatenate([d[:, u * BLK : (u + 1) * BLK] for d in diff], axis=1)


def finish(place, own, met, other, swap):
    both = pl.BlockSpec((NB, 2, PB, TILE), lambda i: (0, 0, i, 0))
    out = pl.pallas_call(
        finish_kernel,
        grid=(32 // PB,),
        out_shape=jax.ShapeDtypeStruct((2, 32, BLK, NB * BLK), F32),
        in_specs=[
            SMEM,
            both,
            pl.BlockSpec((NB, PB, TILE), lambda i: (0, i, 0)),
            both,
            pl.BlockSpec((TILE, TILE), lambda i: (0, 0)),
        ],
        out_specs=pl.BlockSpec((2, PB, BLK, NB * BLK), lambda i: (0, i, 0, 0)),
        compiler_params=pltpu.CompilerParams(vmem_limit_bytes=48 * 2**20),
        name="finish",
    )(place, own, met, other, swap)
    return out.reshape(64, BLK, NB * BLK)


def swap_matrix():
    source = lax.broadcasted_iota(jnp.int32, (TILE, TILE), 0)
    target = lax.broadcasted_iota(jnp.int32, (TILE, TILE), 1)
    return (source % BLK * BLK + source // BLK == target).astype(BF)


def body(amplitudes, integrals, labels, slab_list, block_mask):
    place = jnp.stack([lax.axis_index("row"), lax.axis_index("col")]).astype(jnp.int32)
    swap = swap_matrix()
    there = hop(integrals, "core", 1)
    a0, a1, b0, b1 = cut(place, amplitudes)
    low_a, high_a = ring(a0, a1, "x")
    low_b, high_b = ring(b0, b1, "z")
    av0, av1, bv0, bv1 = stack(low_a + high_a + low_b + high_b)
    low_a, high_a = ring(av0, av1, "z")
    low_b, high_b = ring(bv0, bv1, "x")
    pieces = low_a + high_a + low_b + high_b
    tile = ladder(place, labels, slab_list, block_mask, pieces, integrals, there)
    own = lax.all_to_all(tile, "col", split_axis=0, concat_axis=0, tiled=True)
    other = lax.all_to_all(own, "row", split_axis=0, concat_axis=0, tiled=True)
    met = hop(rest(place, own), "core", 1)
    return finish(place, own, met, other, swap)


def solution(mesh):
    in_specs = (P(None, "col", None), P("row", "col", None, None, None), P(), P(), P())
    out_specs = P("col", "row", None)
    return jax.shard_map(body, mesh=mesh, in_specs=in_specs, out_specs=out_specs, check_vma=False)
```

```python
import jax
import jax.numpy as jnp
from jax import lax
from jax.experimental import pallas as pl
from jax.experimental.pallas import tpu as pltpu
from jax.sharding import PartitionSpec as P

BLK = 32
NSL = 8
CAP = 3
NB = 16
TILE = BLK * BLK
BF = jnp.bfloat16
F32 = jnp.float32
HBM = pl.BlockSpec(memory_space=pltpu.MemorySpace.HBM)
SMEM = pl.BlockSpec(memory_space=pltpu.SMEM)
VM = pl.BlockSpec(memory_space=pltpu.VMEM)
AXES = ("row", "col")
SHIFT = (0, 3, 1, 2)


def hop(array, axis, step):
    pairs = []
    for row in range(NB):
        for col in range(NB):
            y, zh, core, zl, x = row // 4, row // 2 % 2, row % 2, col // 4, col % 4
            z = zh * 4 + zl
            if axis == "x":
                x = (x + step) % 4
            elif axis == "z":
                z = (z + step) % 8
            else:
                core = 1 - core
            to = (y * 4 + z // 4 * 2 + core) * NB + z % 4 * 4 + x
            pairs.append((row * NB + col, to))
    return lax.ppermute(array, AXES, pairs)


def run_copies(copies):
    for copy in copies:
        copy.start()
    for copy in copies:
        copy.wait()


def cut_kernel(place, shard, low, high, sems):
    rows = pl.ds(pl.multiple_of(lax.rem(place[0], 2) * 32, 32), 32)
    run_copies(
        [
            pltpu.make_async_copy(shard.at[half * 4 : half * 4 + 4, rows, :], dst, sems.at[half])
            for half, dst in enumerate((low, high))
        ]
    )


def cut(place, shard):
    return pl.pallas_call(
        cut_kernel,
        out_shape=[jax.ShapeDtypeStruct((4, 32, TILE), BF)] * 2,
        in_specs=[SMEM, HBM],
        out_specs=[VM] * 2,
        scratch_shapes=[pltpu.SemaphoreType.DMA((2,))],
        name="cut",
    )(place, shard)


def stack_kernel(*refs):
    ins, outs, sems = refs[:12], refs[-5:-1], refs[-1]
    run_copies(
        [
            pltpu.make_async_copy(ins[n * 3 + i].at[:, n // 2 * 16 : n // 2 * 16 + 16, :], outs[n].at[i], sems.at[n * 3 + i])
            for n in range(4)
            for i in range(3)
        ]
    )


def stack(pieces, after):
    return pl.pallas_call(
        stack_kernel,
        out_shape=[jax.ShapeDtypeStruct((3, 4, 16, TILE), BF)] * 4,
        in_specs=[HBM] * 13,
        out_specs=[VM] * 4,
        scratch_shapes=[pltpu.SemaphoreType.DMA((12,))],
        name="stack",
    )(*pieces, after)


def ring(a0, a1, axis):
    a0p, a1m = hop(a0, axis, 1), hop(a1, axis, -1)
    a1p, a0m = hop(a1, axis, 1), hop(a0, axis, -1)
    a0pp, a1mm = hop(a0p, axis, 1), hop(a1m, axis, -1)
    return (a0, a0p, a0m, a0pp), (a1, a1p, a1m, a1mm)


def slots(row, col, labels, slab_list, block_mask):
    sym = lax.bitwise_xor(labels[row], labels[col])
    count = jnp.int32(0)
    ids = [jnp.int32(0)] * CAP
    weights = [jnp.float32(0)] * CAP
    for s in range(NSL):
        left, right = slab_list[s, 0], slab_list[s, 1]
        match = lax.bitwise_xor(labels[left], labels[right]) == sym
        alive = jnp.where(block_mask[left, right] == 1, jnp.float32(1), jnp.float32(0))
        for k in range(CAP):
            here = jnp.logical_and(match, count == k)
            ids[k] = jnp.where(here, jnp.int32(s), ids[k])
            weights[k] = jnp.where(here, alive, weights[k])
        count = count + match.astype(jnp.int32)
    return ids, weights


def ladder_kernel(place, labels, slab_list, block_mask, *refs):
    pieces, (here, there, out, lhs, rhs, acc, sems, more) = (refs[:13], refs[13:26]), refs[26:]
    row, col = place[0], place[1]
    core, zl, x = lax.rem(row, 2), col // 4, lax.rem(col, 4)
    tiles = (core, 1 - core)
    stages = []
    for n, source in enumerate((here, there)):
        ids, weights = slots(row + tiles[n] - core, col, labels, slab_list, block_mask)
        stages += [(n, k, source, ids[k], weights[k] > 0) for k in range(CAP)]

    def parts(n, k, slab, half):
        at, of, dst = lax.rem(slab, 4), pieces[half], lhs.at[n, k]
        moves = [(of[0].at[at], dst.at[0, 0])]
        for i in range(1, 4):
            moves.append((of[i].at[at], dst.at[0, i]))
            moves.append((of[3 + i].at[at], dst.at[i, 0]))
            moves.append((of[6 + i].at[:, at], dst.at[i, 1:4, 0:16]))
            moves.append((of[9 + i].at[:, at], dst.at[1:4, i, 16:32]))
        first = (n * CAP + k) * 13
        return [pltpu.make_async_copy(src, to, sems.at[first + i]) for i, (src, to) in enumerate(moves)]

    def start(n, k, source, slab, alive):
        for half in range(2):

            @pl.when(jnp.logical_and(alive, slab // 4 == half))
            def _():
                for copy in parts(n, k, slab, half):
                    copy.start()

        @pl.when(alive)
        def _():
            pltpu.make_async_copy(source.at[0, 0, k], rhs.at[n, k], more.at[n * CAP + k]).start()

    def add(n, k, source, slab, alive):
        @pl.when(alive)
        def _():
            for copy in parts(n, k, slab, 0):
                copy.wait()
            pltpu.make_async_copy(source.at[0, 0, k], rhs.at[n, k], more.at[n * CAP + k]).wait()
            value = lax.dot_general(
                lhs[n, k].reshape(512, TILE),
                rhs[n, k],
                (((1,), (1,)), ((), ())),
                preferred_element_type=F32,
            )
            acc[...] = value if k == 0 else acc[...] + value

        if k == 0:

            @pl.when(jnp.logical_not(alive))
            def _():
                acc[...] = jnp.zeros_like(acc)

    for stage in stages[:2]:
        start(*stage)
    for i, stage in enumerate(stages):
        if i + 2 < len(stages):
            start(*stages[i + 2])
        add(*stage)
        if stage[1] == CAP - 1:
            for rel_z in range(4):
                for rel_x in range(4):
                    q = lax.rem(zl + SHIFT[rel_z], 4) * 4 + lax.rem(x + SHIFT[rel_x], 4)
                    first = (rel_z * 4 + rel_x) * 32
                    out[q, tiles[stage[0]]] = acc[first : first + 32].astype(BF)


def ladder(place, labels, slab_list, block_mask, pieces, here, there):
    return pl.pallas_call(
        ladder_kernel,
        out_shape=jax.ShapeDtypeStruct((NB, 2, 32, TILE), BF),
        in_specs=[SMEM] * 4 + [HBM] * 28,
        out_specs=VM,
        scratch_shapes=[
            pltpu.VMEM((2, CAP, 4, 4, 32, TILE), BF),
            pltpu.VMEM((2, CAP, TILE, TILE), BF),
            pltpu.VMEM((512, TILE), F32),
            pltpu.SemaphoreType.DMA((78,)),
            pltpu.SemaphoreType.DMA((2 * CAP,)),
        ],
        compiler_params=pltpu.CompilerParams(vmem_limit_bytes=60 * 2**20),
        cost_estimate=pl.CostEstimate(flops=6 * 2**30, bytes_accessed=22 * 2**20, transcendentals=0),
        name="ladder",
    )(place, labels, slab_list, block_mask, *pieces, here, there)


def rest_kernel(place, own, out, sem):
    copy = pltpu.make_async_copy(own.at[:, 1 - lax.rem(place[0], 2)], out, sem)
    copy.start()
    copy.wait()


def rest(place, own):
    return pl.pallas_call(
        rest_kernel,
        out_shape=jax.ShapeDtypeStruct((NB, 32, TILE), BF),
        in_specs=[SMEM, HBM],
        out_specs=VM,
        scratch_shapes=[pltpu.SemaphoreType.DMA],
        name="rest",
    )(place, own)


PB = 16


def finish_kernel(place, own, met, other, swap, out):
    core = lax.rem(place[0], 2)
    turned = lax.dot_general(
        other[...].reshape(NB * 2 * PB, TILE),
        swap[...],
        (((1,), (0,)), ((), ())),
        preferred_element_type=F32,
    ).reshape(NB, 2, PB, TILE)
    for half in range(2):
        first = core == half
        diff = []
        for b in range(NB):
            straight = jnp.where(first, own[b, core].astype(F32), met[b].astype(F32))
            diff.append(straight - turned[b // 2 * 2 + half, b % 2])
        for u in range(BLK):
            out[half, :, u, :] = jnp.concatenate([d[:, u * BLK : (u + 1) * BLK] for d in diff], axis=1)


def finish(place, own, met, other, swap):
    both = pl.BlockSpec((NB, 2, PB, TILE), lambda i: (0, 0, i, 0))
    out = pl.pallas_call(
        finish_kernel,
        grid=(32 // PB,),
        out_shape=jax.ShapeDtypeStruct((2, 32, BLK, NB * BLK), F32),
        in_specs=[
            SMEM,
            both,
            pl.BlockSpec((NB, PB, TILE), lambda i: (0, i, 0)),
            both,
            pl.BlockSpec((TILE, TILE), lambda i: (0, 0)),
        ],
        out_specs=pl.BlockSpec((2, PB, BLK, NB * BLK), lambda i: (0, i, 0, 0)),
        compiler_params=pltpu.CompilerParams(vmem_limit_bytes=48 * 2**20),
        name="finish",
    )(place, own, met, other, swap)
    return out.reshape(64, BLK, NB * BLK)


def swap_matrix():
    source = lax.broadcasted_iota(jnp.int32, (TILE, TILE), 0)
    target = lax.broadcasted_iota(jnp.int32, (TILE, TILE), 1)
    return (source % BLK * BLK + source // BLK == target).astype(BF)


def body(amplitudes, integrals, labels, slab_list, block_mask):
    place = jnp.stack([lax.axis_index("row"), lax.axis_index("col")]).astype(jnp.int32)
    swap = swap_matrix()
    there = hop(integrals, "core", 1)
    low, high = cut(place, amplitudes)
    low_x, high_x = ring(low, high, "x")
    low_z, high_z = ring(low, high, "z")
    a0, a1, b0, b1 = stack(low_x[1:] + high_x[1:] + low_z[1:] + high_z[1:], there)
    low_a, high_a = ring(a0, a1, "z")
    low_b, high_b = ring(b0, b1, "x")
    pieces = low_x + low_z[1:] + low_a[1:] + low_b[1:] + high_x + high_z[1:] + high_a[1:] + high_b[1:]
    tile = ladder(place, labels, slab_list, block_mask, pieces, integrals, there)
    own = lax.all_to_all(tile, "col", split_axis=0, concat_axis=0, tiled=True)
    other = lax.all_to_all(own, "row", split_axis=0, concat_axis=0, tiled=True)
    met = hop(rest(place, own), "core", 1)
    return finish(place, own, met, other, swap)


def solution(mesh):
    in_specs = (P(None, "col", None), P("row", "col", None, None, None), P(), P(), P())
    out_specs = P("col", "row", None)
    return jax.shard_map(body, mesh=mesh, in_specs=in_specs, out_specs=out_specs, check_vma=False)
```

```python
import jax
import jax.numpy as jnp
from jax import lax
from jax.experimental import pallas as pl
from jax.experimental.pallas import tpu as pltpu
from jax.sharding import PartitionSpec as P

BLK = 32
NSL = 8
CAP = 3
NB = 16
TILE = BLK * BLK
BF = jnp.bfloat16
F32 = jnp.float32
HBM = pl.BlockSpec(memory_space=pltpu.MemorySpace.HBM)
SMEM = pl.BlockSpec(memory_space=pltpu.SMEM)
VM = pl.BlockSpec(memory_space=pltpu.VMEM)
AXES = ("row", "col")
SHIFT = (0, 3, 1, 2)


def hop(array, axis, step=1):
    pairs = []
    for row in range(NB):
        for col in range(NB):
            y, h, core, l, x = row // 4, row // 2 % 2, row % 2, col // 4, col % 4
            z = h * 4 + l
            if axis == "x":
                x = (x + step) % 4
            elif axis == "z":
                z = (z + (step if step != 2 or z % 2 == 0 else -2)) % 8
            else:
                core = 1 - core
            to = (y * 4 + z // 4 * 2 + core) * NB + z % 4 * 4 + x
            pairs.append((row * NB + col, to))
    return lax.ppermute(array, AXES, pairs)


def run_copies(copies):
    for copy in copies:
        copy.start()
    for copy in copies:
        copy.wait()


def cut_kernel(place, shard, out, sem):
    rows = pl.ds(pl.multiple_of(lax.rem(place[0], 2) * 32, 32), 32)
    run_copies([pltpu.make_async_copy(shard.at[:, rows, :], out, sem)])


def cut(place, shard):
    return pl.pallas_call(
        cut_kernel,
        out_shape=jax.ShapeDtypeStruct((NSL, 32, TILE), BF),
        in_specs=[SMEM, HBM],
        out_specs=VM,
        scratch_shapes=[pltpu.SemaphoreType.DMA],
        name="cut",
    )(place, shard)


def stack_kernel(*refs):
    outs, sems = refs[-3:-1], refs[-1]
    copies = []
    for n in range(4):
        part, half = n // 2, n % 2
        before, after, low, high = refs[part * 4 : part * 4 + 4]
        slabs, rows = slice(half * 4, half * 4 + 4), slice(part * 16, part * 16 + 16)
        sources = (before.at[slabs, rows, :], after.at[slabs, rows, :], (low, high)[half].at[:, rows, :])
        for i, src in enumerate(sources):
            copies.append(pltpu.make_async_copy(src, outs[part].at[half, i], sems.at[n * 3 + i]))
    run_copies(copies)


def stack(pieces, after):
    return pl.pallas_call(
        stack_kernel,
        out_shape=[jax.ShapeDtypeStruct((2, 3, 4, 16, TILE), BF)] * 2,
        in_specs=[HBM] * 9,
        out_specs=[VM] * 2,
        scratch_shapes=[pltpu.SemaphoreType.DMA((12,))],
        name="stack",
    )(*pieces, after)


def ring(own, axis):
    half = own.shape[0] // 2
    before, after = hop(own, axis, 1), hop(own, axis, -1)
    return [before, after, hop(before[:half], axis, 1), hop(after[half:], axis, -1)]


def slots(row, col, labels, slab_list, block_mask):
    sym = lax.bitwise_xor(labels[row], labels[col])
    count = jnp.int32(0)
    ids = [jnp.int32(0)] * CAP
    weights = [jnp.float32(0)] * CAP
    for s in range(NSL):
        left, right = slab_list[s, 0], slab_list[s, 1]
        match = lax.bitwise_xor(labels[left], labels[right]) == sym
        alive = jnp.where(block_mask[left, right] == 1, jnp.float32(1), jnp.float32(0))
        for k in range(CAP):
            here = jnp.logical_and(match, count == k)
            ids[k] = jnp.where(here, jnp.int32(s), ids[k])
            weights[k] = jnp.where(here, alive, weights[k])
        count = count + match.astype(jnp.int32)
    return ids, weights


def ladder_kernel(place, labels, slab_list, block_mask, *refs):
    line, side, (here, there, out, lhs, rhs, acc, sems, more) = refs[:9], refs[9:17], refs[17:]
    row, col = place[0], place[1]
    core, zl, x = lax.rem(row, 2), col // 4, lax.rem(col, 4)
    tiles = (core, 1 - core)
    stages = []
    for n, source in enumerate((here, there)):
        ids, weights = slots(row + tiles[n] - core, col, labels, slab_list, block_mask)
        stages += [(n, k, source, ids[k], weights[k] > 0) for k in range(CAP)]

    def parts(n, k, slab, half):
        at, dst = lax.rem(slab, 4), lhs.at[n, k]
        moves = [(line[0].at[slab], dst.at[0, 0])]
        for i in range(1, 4):
            if i < 3:
                on_x, on_z = line[i].at[slab], line[4 + i].at[slab]
                by_z, by_x = side[i - 1].at[half, :, at], side[3 + i].at[half, :, at]
            else:
                on_x, on_z = line[3 + half].at[at], line[7 + half].at[at]
                by_z, by_x = side[2 + half].at[0, :, at], side[6 + half].at[0, :, at]
            moves.append((on_x, dst.at[0, i]))
            moves.append((on_z, dst.at[i, 0]))
            moves.append((by_z, dst.at[i, 1:4, 0:16]))
            moves.append((by_x, dst.at[1:4, i, 16:32]))
        return [pltpu.make_async_copy(src, to, sems.at[n * CAP + k]) for src, to in moves]

    def start(n, k, source, slab, alive):
        for half in range(2):

            @pl.when(jnp.logical_and(alive, slab // 4 == half))
            def _():
                for copy in parts(n, k, slab, half):
                    copy.start()

        @pl.when(alive)
        def _():
            pltpu.make_async_copy(source.at[0, 0, k], rhs.at[n, k], more.at[n * CAP + k]).start()

    def add(n, k, source, slab, alive):
        @pl.when(alive)
        def _():
            pltpu.make_async_copy(lhs.at[n, k], lhs.at[n, k], sems.at[n * CAP + k]).wait()
            pltpu.make_async_copy(source.at[0, 0, k], rhs.at[n, k], more.at[n * CAP + k]).wait()
            value = lax.dot_general(
                lhs[n, k].reshape(512, TILE),
                rhs[n, k],
                (((1,), (1,)), ((), ())),
                preferred_element_type=F32,
            )
            acc[...] = value if k == 0 else acc[...] + value

        if k == 0:

            @pl.when(jnp.logical_not(alive))
            def _():
                acc[...] = jnp.zeros_like(acc)

    for stage in stages[:2]:
        start(*stage)
    for i, stage in enumerate(stages):
        if i + 2 < len(stages):
            start(*stages[i + 2])
        add(*stage)
        if stage[1] == CAP - 1:
            for rel_z in range(4):
                for rel_x in range(4):
                    q = lax.rem(zl + SHIFT[rel_z], 4) * 4 + lax.rem(x + SHIFT[rel_x], 4)
                    first = (rel_z * 4 + rel_x) * 32
                    out[q, tiles[stage[0]]] = acc[first : first + 32].astype(BF)


def ladder(place, labels, slab_list, block_mask, pieces, here, there):
    return pl.pallas_call(
        ladder_kernel,
        out_shape=jax.ShapeDtypeStruct((NB, 2, 32, TILE), BF),
        in_specs=[SMEM] * 4 + [HBM] * 19,
        out_specs=VM,
        scratch_shapes=[
            pltpu.VMEM((2, CAP, 4, 4, 32, TILE), BF),
            pltpu.VMEM((2, CAP, TILE, TILE), BF),
            pltpu.VMEM((512, TILE), F32),
            pltpu.SemaphoreType.DMA((2 * CAP,)),
            pltpu.SemaphoreType.DMA((2 * CAP,)),
        ],
        compiler_params=pltpu.CompilerParams(vmem_limit_bytes=60 * 2**20),
        cost_estimate=pl.CostEstimate(flops=6 * 2**30, bytes_accessed=22 * 2**20, transcendentals=0),
        name="ladder",
    )(place, labels, slab_list, block_mask, *pieces, here, there)


def rest_kernel(place, own, out, sem):
    copy = pltpu.make_async_copy(own.at[:, 1 - lax.rem(place[0], 2)], out, sem)
    copy.start()
    copy.wait()


def rest(place, own):
    return pl.pallas_call(
        rest_kernel,
        out_shape=jax.ShapeDtypeStruct((NB, 32, TILE), BF),
        in_specs=[SMEM, HBM],
        out_specs=VM,
        scratch_shapes=[pltpu.SemaphoreType.DMA],
        name="rest",
    )(place, own)


PB = 16


def finish_kernel(place, own, met, other, swap, out):
    core = lax.rem(place[0], 2)
    turned = lax.dot_general(
        other[...].reshape(NB * 2 * PB, TILE),
        swap[...],
        (((1,), (0,)), ((), ())),
        preferred_element_type=F32,
    ).reshape(NB, 2, PB, TILE)
    for half in range(2):
        first = core == half
        diff = []
        for b in range(NB):
            straight = jnp.where(first, own[b, core].astype(F32), met[b].astype(F32))
            diff.append(straight - turned[b // 2 * 2 + half, b % 2])
        for u in range(BLK):
            out[half, :, u, :] = jnp.concatenate([d[:, u * BLK : (u + 1) * BLK] for d in diff], axis=1)


def finish(place, own, met, other, swap):
    both = pl.BlockSpec((NB, 2, PB, TILE), lambda i: (0, 0, i, 0))
    out = pl.pallas_call(
        finish_kernel,
        grid=(32 // PB,),
        out_shape=jax.ShapeDtypeStruct((2, 32, BLK, NB * BLK), F32),
        in_specs=[
            SMEM,
            both,
            pl.BlockSpec((NB, PB, TILE), lambda i: (0, i, 0)),
            both,
            pl.BlockSpec((TILE, TILE), lambda i: (0, 0)),
        ],
        out_specs=pl.BlockSpec((2, PB, BLK, NB * BLK), lambda i: (0, i, 0, 0)),
        compiler_params=pltpu.CompilerParams(vmem_limit_bytes=48 * 2**20),
        name="finish",
    )(place, own, met, other, swap)
    return out.reshape(64, BLK, NB * BLK)


def swap_matrix():
    source = lax.broadcasted_iota(jnp.int32, (TILE, TILE), 0)
    target = lax.broadcasted_iota(jnp.int32, (TILE, TILE), 1)
    return (source % BLK * BLK + source // BLK == target).astype(BF)


def body(amplitudes, integrals, labels, slab_list, block_mask):
    place = jnp.stack([lax.axis_index("row"), lax.axis_index("col")]).astype(jnp.int32)
    swap = swap_matrix()
    there = hop(integrals, "core", 1)
    mine = cut(place, amplitudes)
    line = ring(mine, "x") + ring(mine, "z")
    a, b = stack(line, there)
    pieces = [mine, *line, *ring(a, "z"), *ring(b, "x")]
    tile = ladder(place, labels, slab_list, block_mask, pieces, integrals, there)
    own = lax.all_to_all(tile, "col", split_axis=0, concat_axis=0, tiled=True)
    other = lax.all_to_all(own, "row", split_axis=0, concat_axis=0, tiled=True)
    met = hop(rest(place, own), "core", 1)
    return finish(place, own, met, other, swap)


def solution(mesh):
    in_specs = (P(None, "col", None), P("row", "col", None, None, None), P(), P(), P())
    out_specs = P("col", "row", None)
    return jax.shard_map(body, mesh=mesh, in_specs=in_specs, out_specs=out_specs, check_vma=False)
```

```python
import jax
import jax.numpy as jnp
from jax import lax
from jax.experimental import pallas as pl
from jax.experimental.pallas import tpu as pltpu
from jax.sharding import PartitionSpec as P

BLK = 32
NSL = 8
CAP = 3
NB = 16
TILE = BLK * BLK
BF = jnp.bfloat16
F32 = jnp.float32
HBM = pl.BlockSpec(memory_space=pltpu.MemorySpace.HBM)
SMEM = pl.BlockSpec(memory_space=pltpu.SMEM)
VM = pl.BlockSpec(memory_space=pltpu.VMEM)
AXES = ("row", "col")
SHIFT = (0, 3, 1, 2)


def hop(array, axis, step=1):
    pairs = []
    for row in range(NB):
        for col in range(NB):
            y, h, core, l, x = row // 4, row // 2 % 2, row % 2, col // 4, col % 4
            z = h * 4 + l
            if axis == "x":
                x = (x + step) % 4
            elif axis == "z":
                z = (z + (step if step != 2 or z % 2 == 0 else -2)) % 8
            else:
                core = 1 - core
            to = (y * 4 + z // 4 * 2 + core) * NB + z % 4 * 4 + x
            pairs.append((row * NB + col, to))
    return lax.ppermute(array, AXES, pairs)


def run_copies(copies):
    for copy in copies:
        copy.start()
    for copy in copies:
        copy.wait()


def stack_kernel(*refs):
    outs, sems = refs[-3:-1], refs[-1]
    copies = []
    for n in range(4):
        part, half = n // 2, n % 2
        before, after, low, high = refs[part * 4 : part * 4 + 4]
        slabs, rows = slice(half * 4, half * 4 + 4), slice(part * 16, part * 16 + 16)
        sources = (before.at[slabs, rows, :], after.at[slabs, rows, :], (low, high)[half].at[:, rows, :])
        for i, src in enumerate(sources):
            copies.append(pltpu.make_async_copy(src, outs[part].at[half, i], sems.at[n * 3 + i]))
    run_copies(copies)


def stack(pieces, after):
    return pl.pallas_call(
        stack_kernel,
        out_shape=[jax.ShapeDtypeStruct((2, 3, 4, 16, TILE), BF)] * 2,
        in_specs=[HBM] * 9,
        out_specs=[VM] * 2,
        scratch_shapes=[pltpu.SemaphoreType.DMA((12,))],
        name="stack",
    )(*pieces, after)


def ring(own, axis):
    half = own.shape[0] // 2
    before, after = hop(own, axis, 1), hop(own, axis, -1)
    return [before, after, hop(before[:half], axis, 1), hop(after[half:], axis, -1)]


def slots(row, col, labels, slab_list, block_mask):
    sym = lax.bitwise_xor(labels[row], labels[col])
    count = jnp.int32(0)
    ids = [jnp.int32(0)] * CAP
    weights = [jnp.float32(0)] * CAP
    for s in range(NSL):
        left, right = slab_list[s, 0], slab_list[s, 1]
        match = lax.bitwise_xor(labels[left], labels[right]) == sym
        alive = jnp.where(block_mask[left, right] == 1, jnp.float32(1), jnp.float32(0))
        for k in range(CAP):
            here = jnp.logical_and(match, count == k)
            ids[k] = jnp.where(here, jnp.int32(s), ids[k])
            weights[k] = jnp.where(here, alive, weights[k])
        count = count + match.astype(jnp.int32)
    return ids, weights


def ladder_kernel(place, labels, slab_list, block_mask, *refs):
    line, side, (here, there, out, lhs, rhs, acc, sems, more) = refs[:9], refs[9:17], refs[17:]
    row, col = place[0], place[1]
    core, zl, x = lax.rem(row, 2), col // 4, lax.rem(col, 4)
    tiles = (core, 1 - core)
    stages = []
    for n, source in enumerate((here, there)):
        ids, weights = slots(row + tiles[n] - core, col, labels, slab_list, block_mask)
        stages += [(n, k, source, ids[k], weights[k] > 0) for k in range(CAP)]

    def parts(n, k, slab, half):
        at, dst = lax.rem(slab, 4), lhs.at[n, k]
        moves = [(line[0].at[slab], dst.at[0, 0])]
        for i in range(1, 4):
            if i < 3:
                on_x, on_z = line[i].at[slab], line[4 + i].at[slab]
                by_z, by_x = side[i - 1].at[half, :, at], side[3 + i].at[half, :, at]
            else:
                on_x, on_z = line[3 + half].at[at], line[7 + half].at[at]
                by_z, by_x = side[2 + half].at[0, :, at], side[6 + half].at[0, :, at]
            moves.append((on_x, dst.at[0, i]))
            moves.append((on_z, dst.at[i, 0]))
            moves.append((by_z, dst.at[i, 1:4, 0:16]))
            moves.append((by_x, dst.at[1:4, i, 16:32]))
        return [pltpu.make_async_copy(src, to, sems.at[n * CAP + k]) for src, to in moves]

    def start(n, k, source, slab, alive):
        for half in range(2):

            @pl.when(jnp.logical_and(alive, slab // 4 == half))
            def _():
                for copy in parts(n, k, slab, half):
                    copy.start()

        @pl.when(alive)
        def _():
            pltpu.make_async_copy(source.at[0, 0, k], rhs.at[n, k], more.at[n * CAP + k]).start()

    def add(n, k, source, slab, alive):
        @pl.when(alive)
        def _():
            pltpu.make_async_copy(lhs.at[n, k], lhs.at[n, k], sems.at[n * CAP + k]).wait()
            pltpu.make_async_copy(source.at[0, 0, k], rhs.at[n, k], more.at[n * CAP + k]).wait()
            value = lax.dot_general(
                lhs[n, k].reshape(512, TILE),
                rhs[n, k],
                (((1,), (1,)), ((), ())),
                preferred_element_type=F32,
            )
            acc[...] = value if k == 0 else acc[...] + value

        if k == 0:

            @pl.when(jnp.logical_not(alive))
            def _():
                acc[...] = jnp.zeros_like(acc)

    for stage in stages[:2]:
        start(*stage)
    for i, stage in enumerate(stages):
        if i + 2 < len(stages):
            start(*stages[i + 2])
        add(*stage)
        if stage[1] == CAP - 1:
            for rel_z in range(4):
                for rel_x in range(4):
                    q = lax.rem(zl + SHIFT[rel_z], 4) * 4 + lax.rem(x + SHIFT[rel_x], 4)
                    first = (rel_z * 4 + rel_x) * 32
                    out[q, tiles[stage[0]]] = acc[first : first + 32].astype(BF)


def ladder(place, labels, slab_list, block_mask, pieces, here, there):
    return pl.pallas_call(
        ladder_kernel,
        out_shape=jax.ShapeDtypeStruct((NB, 2, 32, TILE), BF),
        in_specs=[SMEM] * 4 + [HBM] * 19,
        out_specs=VM,
        scratch_shapes=[
            pltpu.VMEM((2, CAP, 4, 4, 32, TILE), BF),
            pltpu.VMEM((2, CAP, TILE, TILE), BF),
            pltpu.VMEM((512, TILE), F32),
            pltpu.SemaphoreType.DMA((2 * CAP,)),
            pltpu.SemaphoreType.DMA((2 * CAP,)),
        ],
        compiler_params=pltpu.CompilerParams(vmem_limit_bytes=60 * 2**20),
        cost_estimate=pl.CostEstimate(flops=6 * 2**30, bytes_accessed=22 * 2**20, transcendentals=0),
        name="ladder",
    )(place, labels, slab_list, block_mask, *pieces, here, there)


def rest_kernel(place, own, out, sem):
    copy = pltpu.make_async_copy(own.at[:, 1 - lax.rem(place[0], 2)], out, sem)
    copy.start()
    copy.wait()


def rest(place, own):
    return pl.pallas_call(
        rest_kernel,
        out_shape=jax.ShapeDtypeStruct((NB, 32, TILE), BF),
        in_specs=[SMEM, HBM],
        out_specs=VM,
        scratch_shapes=[pltpu.SemaphoreType.DMA],
        name="rest",
    )(place, own)


PB = 16


def finish_kernel(place, own, met, other, swap, out):
    core = lax.rem(place[0], 2)
    turned = lax.dot_general(
        other[...].reshape(NB * 2 * PB, TILE),
        swap[...],
        (((1,), (0,)), ((), ())),
        preferred_element_type=F32,
    ).reshape(NB, 2, PB, TILE)
    for half in range(2):
        first = core == half
        diff = []
        for b in range(NB):
            straight = jnp.where(first, own[b, core].astype(F32), met[b].astype(F32))
            diff.append(straight - turned[b // 2 * 2 + half, b % 2])
        for u in range(BLK):
            out[half, :, u, :] = jnp.concatenate([d[:, u * BLK : (u + 1) * BLK] for d in diff], axis=1)


def finish(place, own, met, other, swap):
    both = pl.BlockSpec((NB, 2, PB, TILE), lambda i: (0, 0, i, 0))
    out = pl.pallas_call(
        finish_kernel,
        grid=(32 // PB,),
        out_shape=jax.ShapeDtypeStruct((2, 32, BLK, NB * BLK), F32),
        in_specs=[
            SMEM,
            both,
            pl.BlockSpec((NB, PB, TILE), lambda i: (0, i, 0)),
            both,
            pl.BlockSpec((TILE, TILE), lambda i: (0, 0)),
        ],
        out_specs=pl.BlockSpec((2, PB, BLK, NB * BLK), lambda i: (0, i, 0, 0)),
        compiler_params=pltpu.CompilerParams(vmem_limit_bytes=48 * 2**20),
        name="finish",
    )(place, own, met, other, swap)
    return out.reshape(64, BLK, NB * BLK)


def swap_matrix():
    source = lax.broadcasted_iota(jnp.int32, (TILE, TILE), 0)
    target = lax.broadcasted_iota(jnp.int32, (TILE, TILE), 1)
    return (source % BLK * BLK + source // BLK == target).astype(BF)


def body(amplitudes, integrals, labels, slab_list, block_mask):
    place = jnp.stack([lax.axis_index("row"), lax.axis_index("col")]).astype(jnp.int32)
    swap = swap_matrix()
    there = hop(integrals, "core", 1)
    mine = lax.dynamic_slice(amplitudes, (0, lax.axis_index("row") % 2 * 32, 0), (NSL, 32, TILE))
    line = ring(mine, "x") + ring(mine, "z")
    a, b = stack(line, there)
    pieces = [mine, *line, *ring(a, "z"), *ring(b, "x")]
    tile = ladder(place, labels, slab_list, block_mask, pieces, integrals, there)
    own = lax.all_to_all(tile, "col", split_axis=0, concat_axis=0, tiled=True)
    other = lax.all_to_all(own, "row", split_axis=0, concat_axis=0, tiled=True)
    met = hop(rest(place, own), "core", 1)
    return finish(place, own, met, other, swap)


def solution(mesh):
    in_specs = (P(None, "col", None), P("row", "col", None, None, None), P(), P(), P())
    out_specs = P("col", "row", None)
    return jax.shard_map(body, mesh=mesh, in_specs=in_specs, out_specs=out_specs, check_vma=False)
```

```python
import jax
import jax.numpy as jnp
from jax import lax
from jax.experimental import pallas as pl
from jax.experimental.pallas import tpu as pltpu
from jax.sharding import PartitionSpec as P

BLK = 32
NSL = 8
CAP = 3
NB = 16
TILE = BLK * BLK
BF = jnp.bfloat16
F32 = jnp.float32
HBM = pl.BlockSpec(memory_space=pltpu.MemorySpace.HBM)
SMEM = pl.BlockSpec(memory_space=pltpu.SMEM)
VM = pl.BlockSpec(memory_space=pltpu.VMEM)
AXES = ("row", "col")
SHIFT = (0, 3, 1, 2)


def hop(array, axis, step=1):
    pairs = []
    for row in range(NB):
        for col in range(NB):
            y, h, core, l, x = row // 4, row // 2 % 2, row % 2, col // 4, col % 4
            z = h * 4 + l
            if axis == "x":
                x = (x + step) % 4
            elif axis == "z":
                z = (z + (step if step != 2 or z % 2 == 0 else -2)) % 8
            else:
                core = 1 - core
            to = (y * 4 + z // 4 * 2 + core) * NB + z % 4 * 4 + x
            pairs.append((row * NB + col, to))
    return lax.ppermute(array, AXES, pairs)


def run_copies(copies):
    for copy in copies:
        copy.start()
    for copy in copies:
        copy.wait()


def stack_kernel(*refs):
    outs, sems = refs[-3:-1], refs[-1]
    copies = []
    for n in range(4):
        part, half = n // 2, n % 2
        before, after, low, high = refs[part * 4 : part * 4 + 4]
        slabs, rows = slice(half * 4, half * 4 + 4), slice(part * 16, part * 16 + 16)
        sources = (before.at[slabs, rows, :], after.at[slabs, rows, :], (low, high)[half].at[:, rows, :])
        for i, src in enumerate(sources):
            copies.append(pltpu.make_async_copy(src, outs[part].at[half, i], sems.at[n * 3 + i]))
    run_copies(copies)


def stack(pieces, after):
    return pl.pallas_call(
        stack_kernel,
        out_shape=[jax.ShapeDtypeStruct((2, 3, 4, 16, TILE), BF)] * 2,
        in_specs=[HBM] * 9,
        out_specs=[VM] * 2,
        scratch_shapes=[pltpu.SemaphoreType.DMA((12,))],
        name="stack",
    )(*pieces, after)


def ring(own, axis):
    half = own.shape[0] // 2
    before, after = hop(own, axis, 1), hop(own, axis, -1)
    return [before, after, hop(before[:half], axis, 1), hop(after[half:], axis, -1)]


def slots(row, col, labels, slab_list, block_mask):
    sym = lax.bitwise_xor(labels[row], labels[col])
    count = jnp.int32(0)
    ids = [jnp.int32(0)] * CAP
    weights = [jnp.float32(0)] * CAP
    for s in range(NSL):
        left, right = slab_list[s, 0], slab_list[s, 1]
        match = lax.bitwise_xor(labels[left], labels[right]) == sym
        alive = jnp.where(block_mask[left, right] == 1, jnp.float32(1), jnp.float32(0))
        for k in range(CAP):
            here = jnp.logical_and(match, count == k)
            ids[k] = jnp.where(here, jnp.int32(s), ids[k])
            weights[k] = jnp.where(here, alive, weights[k])
        count = count + match.astype(jnp.int32)
    return ids, weights


def ladder_kernel(place, labels, slab_list, block_mask, *refs):
    line, side, (here, there, out, lhs, rhs, acc, sems, more) = refs[:9], refs[9:17], refs[17:]
    row, col = place[0], place[1]
    core, zl, x = lax.rem(row, 2), col // 4, lax.rem(col, 4)
    tiles = (core, 1 - core)
    stages = []
    for n, source in enumerate((here, there)):
        ids, weights = slots(row + tiles[n] - core, col, labels, slab_list, block_mask)
        stages += [(n, k, source, ids[k], weights[k] > 0) for k in range(CAP)]

    def parts(n, k, slab, half):
        at, dst = lax.rem(slab, 4), lhs.at[n, k]
        moves = [(line[0].at[slab], dst.at[0, 0])]
        for i in range(1, 4):
            if i < 3:
                on_x, on_z = line[i].at[slab], line[4 + i].at[slab]
                by_z, by_x = side[i - 1].at[half, :, at], side[3 + i].at[half, :, at]
            else:
                on_x, on_z = line[3 + half].at[at], line[7 + half].at[at]
                by_z, by_x = side[2 + half].at[0, :, at], side[6 + half].at[0, :, at]
            moves.append((on_x, dst.at[0, i]))
            moves.append((on_z, dst.at[i, 0]))
            moves.append((by_z, dst.at[i, 1:4, 0:16]))
            moves.append((by_x, dst.at[1:4, i, 16:32]))
        return [pltpu.make_async_copy(src, to, sems.at[n * CAP + k]) for src, to in moves]

    def start(n, k, source, slab, alive):
        for half in range(2):

            @pl.when(jnp.logical_and(alive, slab // 4 == half))
            def _():
                for copy in parts(n, k, slab, half):
                    copy.start()

        @pl.when(alive)
        def _():
            pltpu.make_async_copy(source.at[0, 0, k], rhs.at[n, k], more.at[n * CAP + k]).start()

    def add(n, k, source, slab, alive):
        @pl.when(alive)
        def _():
            pltpu.make_async_copy(lhs.at[n, k], lhs.at[n, k], sems.at[n * CAP + k]).wait()
            pltpu.make_async_copy(source.at[0, 0, k], rhs.at[n, k], more.at[n * CAP + k]).wait()
            value = lax.dot_general(
                lhs[n, k].reshape(512, TILE),
                rhs[n, k],
                (((1,), (1,)), ((), ())),
                preferred_element_type=F32,
            )
            acc[...] = value if k == 0 else acc[...] + value

        if k == 0:

            @pl.when(jnp.logical_not(alive))
            def _():
                acc[...] = jnp.zeros_like(acc)

    for stage in stages[:3]:
        start(*stage)
    for i, stage in enumerate(stages):
        if i + 3 < len(stages):
            start(*stages[i + 3])
        add(*stage)
        if stage[1] == CAP - 1:
            for rel_z in range(4):
                for rel_x in range(4):
                    q = lax.rem(zl + SHIFT[rel_z], 4) * 4 + lax.rem(x + SHIFT[rel_x], 4)
                    first = (rel_z * 4 + rel_x) * 32
                    out[q, tiles[stage[0]]] = acc[first : first + 32].astype(BF)


def ladder(place, labels, slab_list, block_mask, pieces, here, there):
    return pl.pallas_call(
        ladder_kernel,
        out_shape=jax.ShapeDtypeStruct((NB, 2, 32, TILE), BF),
        in_specs=[SMEM] * 4 + [HBM] * 19,
        out_specs=VM,
        scratch_shapes=[
            pltpu.VMEM((2, CAP, 4, 4, 32, TILE), BF),
            pltpu.VMEM((2, CAP, TILE, TILE), BF),
            pltpu.VMEM((512, TILE), F32),
            pltpu.SemaphoreType.DMA((2 * CAP,)),
            pltpu.SemaphoreType.DMA((2 * CAP,)),
        ],
        compiler_params=pltpu.CompilerParams(vmem_limit_bytes=60 * 2**20),
        cost_estimate=pl.CostEstimate(flops=6 * 2**30, bytes_accessed=22 * 2**20, transcendentals=0),
        name="ladder",
    )(place, labels, slab_list, block_mask, *pieces, here, there)


def rest_kernel(place, own, out, sem):
    copy = pltpu.make_async_copy(own.at[:, 1 - lax.rem(place[0], 2)], out, sem)
    copy.start()
    copy.wait()


def rest(place, own):
    return pl.pallas_call(
        rest_kernel,
        out_shape=jax.ShapeDtypeStruct((NB, 32, TILE), BF),
        in_specs=[SMEM, HBM],
        out_specs=VM,
        scratch_shapes=[pltpu.SemaphoreType.DMA],
        name="rest",
    )(place, own)


PB = 16


def finish_kernel(place, own, met, other, swap, out):
    core = lax.rem(place[0], 2)
    turned = lax.dot_general(
        other[...].reshape(NB * 2 * PB, TILE),
        swap[...],
        (((1,), (0,)), ((), ())),
        preferred_element_type=F32,
    ).reshape(NB, 2, PB, TILE)
    for half in range(2):
        first = core == half
        diff = []
        for b in range(NB):
            straight = jnp.where(first, own[b, core].astype(F32), met[b].astype(F32))
            diff.append(straight - turned[b // 2 * 2 + half, b % 2])
        for u in range(BLK):
            out[half, :, u, :] = jnp.concatenate([d[:, u * BLK : (u + 1) * BLK] for d in diff], axis=1)


def finish(place, own, met, other, swap):
    both = pl.BlockSpec((NB, 2, PB, TILE), lambda i: (0, 0, i, 0))
    out = pl.pallas_call(
        finish_kernel,
        grid=(32 // PB,),
        out_shape=jax.ShapeDtypeStruct((2, 32, BLK, NB * BLK), F32),
        in_specs=[
            SMEM,
            both,
            pl.BlockSpec((NB, PB, TILE), lambda i: (0, i, 0)),
            both,
            pl.BlockSpec((TILE, TILE), lambda i: (0, 0)),
        ],
        out_specs=pl.BlockSpec((2, PB, BLK, NB * BLK), lambda i: (0, i, 0, 0)),
        compiler_params=pltpu.CompilerParams(vmem_limit_bytes=48 * 2**20),
        name="finish",
    )(place, own, met, other, swap)
    return out.reshape(64, BLK, NB * BLK)


def swap_matrix():
    source = lax.broadcasted_iota(jnp.int32, (TILE, TILE), 0)
    target = lax.broadcasted_iota(jnp.int32, (TILE, TILE), 1)
    return (source % BLK * BLK + source // BLK == target).astype(BF)


def body(amplitudes, integrals, labels, slab_list, block_mask):
    place = jnp.stack([lax.axis_index("row"), lax.axis_index("col")]).astype(jnp.int32)
    swap = swap_matrix()
    there = hop(integrals, "core", 1)
    mine = lax.dynamic_slice(amplitudes, (0, lax.axis_index("row") % 2 * 32, 0), (NSL, 32, TILE))
    line = ring(mine, "x") + ring(mine, "z")
    a, b = stack(line, there)
    pieces = [mine, *line, *ring(a, "z"), *ring(b, "x")]
    tile = ladder(place, labels, slab_list, block_mask, pieces, integrals, there)
    own = lax.all_to_all(tile, "col", split_axis=0, concat_axis=0, tiled=True)
    other = lax.all_to_all(own, "row", split_axis=0, concat_axis=0, tiled=True)
    met = hop(rest(place, own), "core", 1)
    return finish(place, own, met, other, swap)


def solution(mesh):
    in_specs = (P(None, "col", None), P("row", "col", None, None, None), P(), P(), P())
    out_specs = P("col", "row", None)
    return jax.shard_map(body, mesh=mesh, in_specs=in_specs, out_specs=out_specs, check_vma=False)
```
